32 devices in a mesh: survey: 2 (over y), slab: 16 (over z, x, core).
Axes of the slice: x: 2, y: 2, z: 4, core: 2. Of those that a mesh axis runs over, the one named last changes fastest.
Arguments:
- cond: float32 [128, 128, 128], P(('survey', 'slab')), parts along dimension 0, may hold values from 0.3 to 3
- currents: float32 [2, 1024], P('survey'), parts along dimension 0, may hold values from -24 to 24
- source_planes: int32 [2, 1024], P('survey'), parts along dimension 0, may hold values from 0 to 63
- source_spots: int32 [2, 1024], P('survey'), parts along dimension 0, may hold values from 0 to 16383
- data: float32 [2, 2048], P('survey'), parts along dimension 0, may hold values from -6 to 6
- receiver_planes: int32 [2, 2048], P('survey'), parts along dimension 0, may hold values from 0 to 63
- receiver_spots: int32 [2, 2048], P('survey'), parts along dimension 0, may hold values from 0 to 16383
Outputs:
- potential: float32 [2, 64, 128, 128], P('survey', 'slab'), parts along dimension 0
- gradient: float32 [128, 128, 128], P(('survey', 'slab')), parts along dimension 0
The draws below stay inside these ranges and needn't reach their ends.
There are 2 independent parts, one for each index of `survey`. The reference program is written for one: setup_inputs(seed, part) draws one part's arguments, and reference() takes and returns one part's arrays. A program takes and returns all parts, laid end to end along the dimension named above; each array names one. Nothing has to cross between parts.
Inputs may be any that keep to these rules, and one draw needn't show every extreme that they name: `source_planes`: entries may repeat. `receiver_planes`: entries may repeat.
All inputs are finite; a program needn't handle non-finite values.
Results may differ from the reference program's by a relative error of at most 0.0003.
Values sent between devices are 32-bit elements; how exact they have to be, the bound alone decides.
A program may use at most 64 MiB of HBM per device.

```python
import math
import jax
import jax.numpy as jnp
from jax import lax

NY = 128
NZ = 128
SRC = 1
ELEC = 1024
RECV = 2048
NX = 64


def touch_ends(result, own_key, smallest, high):
    shape = result.shape
    place = [jax.random.randint(jax.random.fold_in(own_key, axis), (), 0, shape[axis]) for axis in range(len(shape))]
    result = result.at[tuple(place)].set(smallest)
    longest = shape.index(max(shape))
    place[longest] = (place[longest] + 1) % shape[longest]
    return result.at[tuple(place)].set(high)


def level_of(rng, dims, split, low, high):
    def one(axis_at, blocks):
        heights = jax.random.uniform(jax.random.fold_in(jax.random.fold_in(rng, 6), axis_at), (blocks,), jnp.float32, low / len(split), high / len(split))
        return jnp.repeat(jnp.exp(heights), dims[axis_at] // blocks).reshape((-1,) + (1,) * (len(dims) - axis_at - 1))

    gain = one(*split[0])
    for cut in split[1:]:
        gain = gain * one(*cut)
    return gain


def bell_draw(stream_key, dims, deviation, limit, held_as=jnp.bfloat16):
    return jnp.clip(deviation * jax.random.normal(stream_key, dims, jnp.float32), -limit, limit).astype(held_as)


def setup_inputs(seed: int = 0, part: int = 0) -> dict:
    key_of = jax.random.split(jax.random.key(seed), 8)
    part_splits = jax.random.split(jax.random.fold_in(key_of[7], part), 8)
    cond = jnp.clip(jnp.exp(math.log(3.0) - 2.3025851 * jax.random.uniform(part_splits[0], (NX, NY, NZ), jnp.float32) ** level_of(part_splits[0], (NX, NY, NZ), ((0, 16),), -0.2, 0.2)), 0.3, 3.0)
    currents = bell_draw(part_splits[1], (SRC, ELEC), 4.0, 24.0, jnp.float32)
    source_planes = touch_ends(jax.random.randint(part_splits[2], (SRC, ELEC), 0, NX), jax.random.fold_in(part_splits[2], 1), 0, NX - 1).astype(jnp.int32)
    source_spots = touch_ends(jax.random.randint(part_splits[3], (SRC, ELEC), 0, NY * NZ), jax.random.fold_in(part_splits[3], 1), 0, (NY * NZ) - 1).astype(jnp.int32)
    data = bell_draw(part_splits[4], (SRC, RECV), 1.0, 6.0, jnp.float32)
    receiver_planes = touch_ends(jax.random.randint(part_splits[5], (SRC, RECV), 0, NX), jax.random.fold_in(part_splits[5], 1), 0, NX - 1).astype(jnp.int32)
    receiver_spots = touch_ends(jax.random.randint(part_splits[6], (SRC, RECV), 0, NY * NZ), jax.random.fold_in(part_splits[6], 1), 0, (NY * NZ) - 1).astype(jnp.int32)
    return dict(cond=cond, currents=currents, source_planes=source_planes, source_spots=source_spots, data=data, receiver_planes=receiver_planes, receiver_spots=receiver_spots)


smooth_weight = 2.0 / 3.0
coarse_scale = 16.0

def sine_table(count):
    order = jnp.arange(count, dtype=jnp.float32) + 1.0
    return jnp.sqrt(2.0 / (count + 1.0)) * jnp.sin(jnp.pi * order[:, None] * order[None, :] / (count + 1.0))

def mode_roots(count):
    order = jnp.arange(count, dtype=jnp.float32) + 1.0
    return 2.0 - 2.0 * jnp.cos(jnp.pi * order / (count + 1.0))

def face_terms(cond):
    padded = jnp.pad(cond, 1)
    face_x = 0.5 * (padded[1:, 1:-1, 1:-1] + padded[:-1, 1:-1, 1:-1])
    face_y = 0.5 * (padded[1:-1, 1:, 1:-1] + padded[1:-1, :-1, 1:-1])
    face_z = 0.5 * (padded[1:-1, 1:-1, 1:] + padded[1:-1, 1:-1, :-1])
    diagonal = face_x[:-1] + face_x[1:] + face_y[:, :-1] + face_y[:, 1:] + face_z[:, :, :-1] + face_z[:, :, 1:]
    return ((face_x, face_y, face_z), diagonal)

def apply_operator(values, face_set):
    face_x, face_y, face_z = face_set
    padded = jnp.pad(values, 1)
    flux_x = face_x * (padded[1:, 1:-1, 1:-1] - padded[:-1, 1:-1, 1:-1])
    flux_y = face_y * (padded[1:-1, 1:, 1:-1] - padded[1:-1, :-1, 1:-1])
    flux_z = face_z * (padded[1:-1, 1:-1, 1:] - padded[1:-1, 1:-1, :-1])
    return flux_x[:-1] - flux_x[1:] + (flux_y[:, :-1] - flux_y[:, 1:]) + (flux_z[:, :, :-1] - flux_z[:, :, 1:])

def coarse_solve(coarse):
    planes, rows_y, rows_z = coarse.shape
    table_y = sine_table(rows_y)
    table_z = sine_table(rows_z)
    spectra = jnp.einsum('jy,xyz,kz->xjk', table_y, coarse, table_z, precision=lax.Precision.HIGHEST)
    diag_modes = coarse_scale * (2.0 + mode_roots(rows_y)[:, None] + mode_roots(rows_z)[None, :])
    stacked = spectra.reshape(planes, rows_y * rows_z).T
    position = jnp.arange(planes)
    lower_band = jnp.broadcast_to(jnp.where(position == 0, 0.0, -coarse_scale), stacked.shape).astype(stacked.dtype)
    upper_band = jnp.broadcast_to(jnp.where(position == planes - 1, 0.0, -coarse_scale), stacked.shape).astype(stacked.dtype)
    diagonal = jnp.broadcast_to(diag_modes.reshape(-1)[:, None], stacked.shape).astype(stacked.dtype)
    solved = lax.linalg.tridiagonal_solve(lower_band, diagonal, upper_band, stacked[..., None])[..., 0]
    spatial = solved.T.reshape(planes, rows_y, rows_z)
    return jnp.einsum('jy,xjk,kz->xyz', table_y, spatial, table_z, precision=lax.Precision.HIGHEST)

def precondition(residual, face_set, diagonal):
    extent = residual.shape
    smoothed = smooth_weight * residual / diagonal
    remaining = residual - apply_operator(smoothed, face_set)
    blocks = (extent[0] // 4, 4, extent[1] // 4, 4, extent[2] // 4, 4)
    coarse = remaining.reshape(blocks).sum(axis=(1, 3, 5))
    correction = coarse_solve(coarse)
    lifted = jnp.broadcast_to(correction[:, None, :, None, :, None], blocks).reshape(extent)
    second = smoothed + lifted
    return second + smooth_weight * (residual - apply_operator(second, face_set)) / diagonal

def one_step(source, face_set, diagonal):
    precond = precondition(source, face_set, diagonal)
    image = apply_operator(precond, face_set)
    step_size = jnp.sum(source * precond) / jnp.sum(precond * image)
    return step_size * precond

def reference(cond, currents, source_planes, source_spots, data, receiver_planes, receiver_spots):
    face_set, diagonal = face_terms(cond)
    extent = cond.shape
    total = extent[0] * extent[1] * extent[2]
    plane_total = extent[1] * extent[2]

    def per_source(inputs):
        current_row, src_plane, src_spot, data_row, recv_plane, recv_spot = inputs
        source_row = (src_plane * plane_total + src_spot).astype(jnp.int32)
        receiver_row = (recv_plane * plane_total + recv_spot).astype(jnp.int32)
        forcing = jnp.zeros((total,), cond.dtype).at[source_row].add(current_row).reshape(extent)
        forward = one_step(forcing, face_set, diagonal)
        misfit = forward.reshape(-1)[receiver_row] - data_row
        adjoint_rhs = jnp.zeros((total,), cond.dtype).at[receiver_row].add(misfit).reshape(extent)
        adjoint = one_step(adjoint_rhs, face_set, diagonal)
        pad_f = jnp.pad(forward, 1)
        pad_a = jnp.pad(adjoint, 1)
        prod_x = (pad_f[1:, 1:-1, 1:-1] - pad_f[:-1, 1:-1, 1:-1]) * (pad_a[1:, 1:-1, 1:-1] - pad_a[:-1, 1:-1, 1:-1])
        prod_y = (pad_f[1:-1, 1:, 1:-1] - pad_f[1:-1, :-1, 1:-1]) * (pad_a[1:-1, 1:, 1:-1] - pad_a[1:-1, :-1, 1:-1])
        prod_z = (pad_f[1:-1, 1:-1, 1:] - pad_f[1:-1, 1:-1, :-1]) * (pad_a[1:-1, 1:-1, 1:] - pad_a[1:-1, 1:-1, :-1])
        cells = prod_x[:-1] + prod_x[1:] + prod_y[:, :-1] + prod_y[:, 1:] + prod_z[:, :, :-1] + prod_z[:, :, 1:]
        return (forward, -0.5 * cells)
    forward, terms = lax.map(per_source, (currents, source_planes, source_spots, data, receiver_planes, receiver_spots))
    return (forward, lax.optimization_barrier(jnp.sum(terms, axis=0)))
```

```python
import functools

import jax
import jax.numpy as jnp
import numpy as np
from jax import lax
from jax.experimental import pallas as pl
from jax.experimental.pallas import tpu as pltpu
from jax.sharding import PartitionSpec as P

DEPTH = 4
SIDE = 128
COARSE = 32
BF16 = jnp.bfloat16
F32 = jnp.float32
NT = (((1,), (1,)), ((), ()))


def split_np(table, axis, lead):
    high = table.astype(jnp.bfloat16)
    low = (table - high.astype(np.float64)).astype(jnp.bfloat16)
    return np.concatenate([high, high, low], axis=axis)


def tables(n):
    order = np.arange(COARSE, dtype=np.float64) + 1.0
    sine = np.sqrt(2.0 / (COARSE + 1.0)) * np.sin(
        np.pi * order[:, None] * order[None, :] / (COARSE + 1.0)
    )
    fine = np.repeat(sine, 4, axis=1)
    forward_y = split_np(fine, 1, 0)
    forward_z = split_np(np.tile(fine.T, (1, 4)), 0, 0)
    inverse_z = split_np(np.tile(fine, (4, 1)), 0, 0)
    inverse_y = split_np(fine.T, 1, 0)
    roots = 2.0 - 2.0 * np.cos(np.pi * order / (COARSE + 1.0))
    half = (2.0 + roots[:, None] + roots[None, :]) / 2.0
    theta = np.arccosh(half)
    scale = 1.0 / (
        16.0 * 2.0 * np.sinh(theta) * (-np.expm1(-(2.0 * n + 2.0) * theta))
    )
    pack = lambda a: a.reshape(4, 8, COARSE).transpose(1, 0, 2).reshape(8, SIDE)
    modes = np.stack([pack(theta), pack(scale)]).astype(np.float32)
    return forward_y, forward_z, inverse_z, inverse_y, modes


def pieces(value, axis):
    high = value.astype(BF16)
    low = (value - high.astype(F32)).astype(BF16)
    return jnp.concatenate([high, low, high], axis=axis)


def dot(a, b, dims=(((1,), (0,)), ((), ()))):
    return lax.dot_general(a, b, dims, preferred_element_type=F32)


def kernel(
    n,
    cond_h, cur_h, sp_h, ss_h, dat_h, rp_h, rs_h, fy_h, fz_h, iz_h, iy_h, mode_h,
    zf_o, grad_o, scal_o,
    cond, cur, sp, ss, dat, rp, rs, fy, fz, iz, iy, mode,
    mask_s, mask_r, sx, sy, sz, dg, w, r, cnt, dd, x1, x2, ru, za, zfull, weight,
    spec_f, spec_d, spec_u, sum_a, sum_b,
    got_f, got_d, got_u, got_a, got_b,
    local_sem, halo_send, halo_recv, send_sem, recv_sem,
):
    me = lax.axis_index("slab")
    peers = n - 1

    def each(body):
        if n <= 16:
            for k in range(1, n):
                body(k)
        else:
            pl.loop(1, n)(body)

    def peer(k):
        return {"slab": lax.rem(me + k, n)}

    barrier = pltpu.get_barrier_semaphore()
    each(lambda k: pl.semaphore_signal(barrier, inc=1, device_id=peer(k)))

    small = [(cur_h, cur), (sp_h, sp), (ss_h, ss), (rp_h, rp), (rs_h, rs), (dat_h, dat),
             (fy_h, fy), (fz_h, fz), (iz_h, iz), (iy_h, iy), (mode_h, mode)]
    loads = [pltpu.make_async_copy(a, b, local_sem.at[i]) for i, (a, b) in enumerate(small)]
    loads.append(pltpu.make_async_copy(cond_h, cond.at[pl.ds(4, 4)], local_sem.at[11]))
    for load in loads:
        load.start()

    halo = [
        (pl.ds(0, 2), pl.ds(8, 2), me - 1),
        (pl.ds(2, 2), pl.ds(10, 2), me - 1),
        (pl.ds(2, 2), pl.ds(2, 2), me + 1),
        (pl.ds(0, 2), pl.ds(0, 2), me + 1),
    ]

    def halo_copy(i):
        source, target, device = halo[i]
        return pltpu.make_async_remote_copy(
            src_ref=cond_h.at[source], dst_ref=cond.at[target],
            send_sem=halo_send.at[i], recv_sem=halo_recv.at[i],
            device_id={"slab": device},
        )

    has_low = me > 0
    has_high = me < n - 1

    @pl.when(me == 0)
    def _():
        cond[0:4] = jnp.zeros((4, SIDE, SIDE), F32)

    @pl.when(me == n - 1)
    def _():
        cond[8:12] = jnp.zeros((4, SIDE, SIDE), F32)

    row_s = lax.broadcasted_iota(jnp.int32, (SIDE, 1), 0)

    def build(planes, spots, low, count, masks):
        key = (planes[...] - low) * SIDE + lax.shift_right_logical(spots[...], 7)
        for p in range(count):
            masks[p * SIDE:(p + 1) * SIDE, :] = jnp.where(
                row_s + p * SIDE == key, 1.0, 0.0
            ).astype(BF16)
        return row_s == (spots[...] & (SIDE - 1))

    for i in range(3):
        loads[i].wait()
    here = build(sp, ss, me * DEPTH - 3, 10, mask_s)
    high = cur[...].astype(BF16).astype(F32)
    low = cur[...] - high
    columns = jnp.concatenate(
        [jnp.where(here, high, 0.0).astype(BF16), jnp.where(here, low, 0.0).astype(BF16)], axis=0
    )

    pl.semaphore_wait(barrier, peers)

    @pl.when(has_low)
    def _():
        halo_copy(0).start()

    @pl.when(has_high)
    def _():
        halo_copy(2).start()

    @pl.when(has_low)
    def _():
        halo_copy(1).start()

    @pl.when(has_high)
    def _():
        halo_copy(3).start()

    placed = dot(mask_s[...], columns, NT)
    for p in range(10):
        rows = slice(p * SIDE, (p + 1) * SIDE)
        r[p + 1] = placed[rows, 0:SIDE] + placed[rows, SIDE:2 * SIDE]

    for i in range(3, 6):
        loads[i].wait()
    here = build(rp, rs, me * DEPTH - 2, 8, mask_r)
    high = dat[...].astype(BF16).astype(F32)
    low = dat[...] - high
    columns = jnp.concatenate(
        [jnp.where(here, value, 0.0).astype(BF16) for value in (1.0, high, low)], axis=0
    )
    placed = dot(mask_r[...], columns, NT)
    for p in range(8):
        rows = slice(p * SIDE, (p + 1) * SIDE)
        cnt[p + 2] = placed[rows, 0:SIDE]
        dd[p + 2] = placed[rows, SIDE:2 * SIDE] + placed[rows, 2 * SIDE:3 * SIDE]

    for i in range(6, 12):
        loads[i].wait()

    def weigh(k):
        theta, scale = mode[0], mode[1]
        other = me - k
        other = jnp.where(other < 0, other + n, other)
        for t in range(3):
            mine = me + (t - 1)
            lower = jnp.minimum(mine, other)
            upper = jnp.maximum(mine, other)
            between = (upper - lower).astype(F32)
            below = (2 * (lower + 1)).astype(F32)
            above = (2 * (n - upper)).astype(F32)
            weight[t, k] = (
                scale
                * jnp.exp(-theta * between)
                * (1.0 - jnp.exp(-theta * below))
                * (1.0 - jnp.exp(-theta * above))
            )

    weigh(0)
    each(weigh)

    y_at = lax.broadcasted_iota(jnp.int32, (SIDE, SIDE), 0)
    z_at = lax.broadcasted_iota(jnp.int32, (SIDE, SIDE), 1)
    y_first, y_last = y_at == 0, y_at == SIDE - 1
    z_first, z_last = z_at == 0, z_at == SIDE - 1

    def back(v, axis):
        return pltpu.roll(v, 1, axis)

    def ahead(v, axis):
        return pltpu.roll(v, SIDE - 1, axis)

    def face_x(p):
        sx[p] = 0.5 * (cond[p - 1] + cond[p])

    def cell(p):
        c = cond[p]
        half = 0.5 * c
        prev_y = jnp.where(y_first, 0.0, back(half, 0))
        next_y = jnp.where(y_last, 0.0, ahead(half, 0))
        prev_z = jnp.where(z_first, 0.0, back(half, 1))
        next_z = jnp.where(z_last, 0.0, ahead(half, 1))
        sy[p] = jnp.where(y_first, 0.0, half + prev_y)
        sz[p] = jnp.where(z_first, 0.0, half + prev_z)
        total = sx[p] + sx[p + 1] + (c + prev_y + next_y) + (c + prev_z + next_z)
        if 4 <= p < 8:
            dg[p - 4] = total
            w[p] = (2.0 / 3.0) / total
        else:
            inside = has_low if p < 4 else has_high
            keep = jnp.where(inside, F32(1.0), F32(0.0))
            w[p] = keep * (2.0 / 3.0) / (total + (1.0 - keep))

    def around(v, p):
        mid = v[p]
        in_y, in_z = sy[p], sz[p]
        return (
            sx[p] * v[p - 1] + sx[p + 1] * v[p + 1]
            + (in_y * back(mid, 0) + ahead(in_y * mid, 0))
            + (in_z * back(mid, 1) + ahead(in_z * mid, 1))
        )

    lane_group = lax.broadcasted_iota(jnp.int32, (8, SIDE), 1) // COARSE

    def to_modes(field):
        left = dot(fy[...], pieces(field, 0))
        full = dot(pieces(left, 1), fz[...])
        out = jnp.zeros((8, SIDE), F32)
        for q in range(4):
            out = jnp.where(lane_group == q, full[8 * q:8 * q + 8], out)
        return out

    def from_modes(packed):
        rows = [jnp.where(lane_group == q, one, 0.0) for one in packed for q in range(4)]
        right = dot(pieces(jnp.concatenate(rows, axis=0), 1), iz[...])
        wide = jnp.concatenate([right[COARSE * t:COARSE * (t + 1)] for t in range(3)], axis=1)
        full = dot(iy[...], pieces(wide, 0))
        return [full[:, SIDE * t:SIDE * (t + 1)] for t in range(3)]

    def gather(source, target, number):
        def send(k):
            pltpu.make_async_remote_copy(
                src_ref=source, dst_ref=target.at[k - 1],
                send_sem=send_sem.at[number], recv_sem=recv_sem.at[number],
                device_id=peer(k),
            ).start()

        each(send)

    def arrived(target, number):
        pltpu.make_async_copy(target, target, recv_sem.at[number]).wait()

    def combine(own, target):
        def add(k, total):
            value = target[k - 1]
            return tuple(total[t] + weight[t, k] * value for t in range(3))

        total = tuple(weight[t, 0] * own[...] for t in range(3))
        if n <= 16:
            for k in range(1, n):
                total = add(k, total)
            return total
        return lax.fori_loop(1, n, add, total)

    def plane_of(p):
        return 0 if p < 4 else (1 if p < 8 else 2)

    @pl.when(has_high)
    def _():
        halo_copy(0).wait_recv()

    @pl.when(has_low)
    def _():
        halo_copy(2).wait_recv()

    for p in range(3, 10):
        face_x(p)
    for p in range(3, 9):
        cell(p)
        x1[p] = w[p] * r[p]
    total = None
    for p in range(4, 8):
        part = r[p] * (1.0 / 3.0) + around(x1, p)
        total = part if total is None else total + part
    spec_f[...] = to_modes(total)
    gather(spec_f, got_f, 0)

    for p in range(3, 9):
        x2[p] = w[p] * dd[p]
    total = None
    for p in range(4, 8):
        part = dd[p] * (1.0 / 3.0) + around(x2, p)
        total = part if total is None else total + part
    spec_d[...] = to_modes(total)
    gather(spec_d, got_d, 1)

    @pl.when(has_high)
    def _():
        halo_copy(1).wait_recv()

    @pl.when(has_low)
    def _():
        halo_copy(3).wait_recv()

    for p in (1, 2, 10, 11):
        face_x(p)
    for p in (1, 2, 9, 10):
        cell(p)
        x1[p] = w[p] * r[p]

    arrived(got_f, 0)
    lifted = from_modes(combine(spec_f, got_f))
    for p in range(1, 11):
        x2[p] = x1[p] + lifted[plane_of(p)]
    for p in range(2, 10):
        z = x2[p] * (1.0 / 3.0) + w[p] * (r[p] + around(x2, p))
        zfull[p] = z
        u = cnt[p] * z
        ru[p] = u
        x1[p] = w[p] * u
    total = None
    for p in range(4, 8):
        part = ru[p] * (1.0 / 3.0) + around(x1, p)
        total = part if total is None else total + part
    spec_u[...] = to_modes(total)
    gather(spec_u, got_u, 2)

    def sums(v, source):
        along = bend = None
        for p in range(4, 8):
            z = v[p]
            a = source(p) * z
            b = z * (dg[p - 4] * z - around(v, p))
            along = a if along is None else along + a
            bend = b if bend is None else bend + b
        return jnp.concatenate(
            [jnp.sum(along, axis=0, keepdims=True), jnp.sum(bend, axis=0, keepdims=True)], axis=0
        )

    def ratio(own, target):
        every = own[...] + jnp.sum(target[...], axis=0)
        both = jnp.sum(every, axis=1, keepdims=True)
        return both[0:1] / both[1:2]

    sum_a[...] = sums(zfull, lambda p: r[p])
    gather(sum_a, got_a, 3)
    for p in range(4):
        zf_o[p] = zfull[p + 4]

    arrived(got_d, 1)
    modes_d = combine(spec_d, got_d)
    arrived(got_a, 3)
    alpha = ratio(sum_a, got_a)
    arrived(got_u, 2)
    modes_u = combine(spec_u, got_u)
    lifted = from_modes([alpha * modes_u[t] - modes_d[t] for t in range(3)])
    for p in range(2, 10):
        ra = alpha * ru[p] - dd[p]
        r[p] = ra
        x2[p] = w[p] * ra + lifted[plane_of(p)]
    for p in range(3, 9):
        za[p] = x2[p] * (1.0 / 3.0) + w[p] * (r[p] + around(x2, p))
    sum_b[...] = sums(za, lambda p: r[p])
    gather(sum_b, got_b, 4)

    def face_pairs(f, a, first, last, axis):
        step_f = f - jnp.where(first, 0.0, back(f, axis))
        step_a = a - jnp.where(first, 0.0, back(a, axis))
        product = step_f * step_a
        return product + jnp.where(last, f * a, ahead(product, axis))

    lower = (zfull[4] - zfull[3]) * (za[4] - za[3])
    for p in range(4, 8):
        f, a = zfull[p], za[p]
        upper = (zfull[p + 1] - f) * (za[p + 1] - a)
        grad_o[p - 4] = (
            lower + upper
            + face_pairs(f, a, y_first, y_last, 0)
            + face_pairs(f, a, z_first, z_last, 1)
        )
        lower = upper

    @pl.when(has_low)
    def _():
        halo_copy(0).wait_send()
        halo_copy(1).wait_send()

    @pl.when(has_high)
    def _():
        halo_copy(2).wait_send()
        halo_copy(3).wait_send()

    for number, target in enumerate((got_f, got_d, got_u, got_a)):
        pltpu.make_async_copy(target, target, send_sem.at[number]).wait()
    arrived(got_b, 4)
    beta = ratio(sum_b, got_b)
    at = lax.broadcasted_iota(jnp.int32, (8, SIDE), 0)
    scal_o[...] = jnp.where(at == 0, alpha, -0.5 * alpha * beta)
    pltpu.make_async_copy(got_b, got_b, send_sem.at[4]).wait()


def on_device(n, cond, *rest):
    elec, recv = rest[0].shape[1], rest[3].shape[1]
    consts = tables(n)
    cube = lambda count: pltpu.VMEM((count, SIDE, SIDE), F32)
    vreg = pltpu.VMEM((8, SIDE), F32)
    pair = pltpu.VMEM((2, SIDE), F32)
    field = jax.ShapeDtypeStruct((DEPTH, SIDE, SIDE), F32)
    scratch = (
        [cube(12)]
        + [pltpu.VMEM(a.shape, a.dtype) for a in rest]
        + [pltpu.VMEM(a.shape, a.dtype) for a in consts]
        + [pltpu.VMEM((10 * SIDE, elec), BF16), pltpu.VMEM((8 * SIDE, recv), BF16)]
        + [cube(12), cube(12), cube(12), cube(4)]
        + [cube(12)] * 9
        + [pltpu.VMEM((3, n, 8, SIDE), F32)]
        + [vreg] * 3 + [pair] * 2
        + [pltpu.VMEM((n - 1, 8, SIDE), F32)] * 3
        + [pltpu.VMEM((n - 1, 2, SIDE), F32)] * 2
        + [
            pltpu.SemaphoreType.DMA((12,)),
            pltpu.SemaphoreType.DMA((4,)),
            pltpu.SemaphoreType.DMA((4,)),
            pltpu.SemaphoreType.DMA((5,)),
            pltpu.SemaphoreType.DMA((5,)),
        ]
    )
    zf, grad, scal = pl.pallas_call(
        functools.partial(kernel, n),
        out_shape=(field, field, jax.ShapeDtypeStruct((8, SIDE), F32)),
        in_specs=[pl.BlockSpec(memory_space=pl.ANY)] * 12,
        out_specs=[pl.BlockSpec(memory_space=pltpu.VMEM)] * 3,
        scratch_shapes=scratch,
        compiler_params=pltpu.CompilerParams(
            collective_id=0, has_side_effects=True, vmem_limit_bytes=48 * 1024 * 1024
        ),
    )(cond, *rest, *[jnp.asarray(c) for c in consts])
    return (scal[0, 0] * zf)[None], scal[1, 0] * grad


def solution(mesh):
    in_specs = (P(("survey", "slab"), None, None),) + (P("survey", None),) * 6
    out_specs = (P("survey", "slab", None, None), P(("survey", "slab"), None, None))
    return jax.shard_map(
        functools.partial(on_device, mesh.shape["slab"]),
        mesh=mesh, in_specs=in_specs, out_specs=out_specs, check_vma=False,
    )
```

```python
import functools

import jax
import jax.numpy as jnp
import numpy as np
from jax import lax
from jax.experimental import pallas as pl
from jax.experimental.pallas import tpu as pltpu
from jax.sharding import PartitionSpec as P

DEPTH = 4
SIDE = 128
COARSE = 32
VMEM_BYTES = 63 * 1024 * 1024
BF16 = jnp.bfloat16
F32 = jnp.float32
NT = (((1,), (1,)), ((), ()))


def split_np(table, axis, lead):
    high = table.astype(jnp.bfloat16)
    low = (table - high.astype(np.float64)).astype(jnp.bfloat16)
    return np.concatenate([high, high, low], axis=axis)


def tables(n):
    order = np.arange(COARSE, dtype=np.float64) + 1.0
    sine = np.sqrt(2.0 / (COARSE + 1.0)) * np.sin(
        np.pi * order[:, None] * order[None, :] / (COARSE + 1.0)
    )
    fine = np.repeat(sine, 4, axis=1)
    forward_y = split_np(fine, 1, 0)
    forward_z = split_np(np.tile(fine.T, (1, 4)), 0, 0)
    inverse_z = split_np(np.tile(fine, (4, 1)), 0, 0)
    inverse_y = split_np(fine.T, 1, 0)
    roots = 2.0 - 2.0 * np.cos(np.pi * order / (COARSE + 1.0))
    half = (2.0 + roots[:, None] + roots[None, :]) / 2.0
    theta = np.arccosh(half)
    scale = 1.0 / (
        16.0 * 2.0 * np.sinh(theta) * (-np.expm1(-(2.0 * n + 2.0) * theta))
    )
    pack = lambda a: a.reshape(4, 8, COARSE).transpose(1, 0, 2).reshape(8, SIDE)
    modes = np.stack([pack(theta), pack(scale)]).astype(np.float32)
    return forward_y, forward_z, inverse_z, inverse_y, modes


def pieces(value, axis):
    high = value.astype(BF16)
    low = (value - high.astype(F32)).astype(BF16)
    return jnp.concatenate([high, low, high], axis=axis)


def dot(a, b, dims=(((1,), (0,)), ((), ()))):
    return lax.dot_general(a, b, dims, preferred_element_type=F32)


def kernel(
    n,
    cond_h, cur_h, sp_h, ss_h, dat_h, rp_h, rs_h, fy_h, fz_h, iz_h, iy_h, mode_h,
    zf_h, grad_h, scal_h,
    cond, cur, sp, ss, dat, rp, rs, fy, fz, iz, iy, mode,
    mask_s, mask_r, sx, sy, sz, dg, w, r, cnt, dd, x1, x2, ru, za, zfull, weight,
    grad_o, scal_o,
    spec_f, spec_d, spec_u, sum_a, sum_b,
    got_f, got_d, got_u, got_a, got_b,
    local_sem, out_sem, halo_send, halo_recv, send_sem, recv_sem,
):
    me = lax.axis_index("slab")
    peers = n - 1

    def each(body):
        if n <= 16:
            for k in range(1, n):
                body(k)
        else:
            pl.loop(1, n)(body)

    def peer(k):
        return {"slab": lax.rem(me + k, n)}

    barrier = pltpu.get_barrier_semaphore()
    each(lambda k: pl.semaphore_signal(barrier, inc=1, device_id=peer(k)))

    small = [(cur_h, cur), (sp_h, sp), (ss_h, ss), (rp_h, rp), (rs_h, rs), (dat_h, dat),
             (fy_h, fy), (fz_h, fz), (iz_h, iz), (iy_h, iy), (mode_h, mode)]
    loads = [pltpu.make_async_copy(a, b, local_sem.at[i]) for i, (a, b) in enumerate(small)]
    loads.append(pltpu.make_async_copy(cond_h, cond.at[pl.ds(4, 4)], local_sem.at[11]))
    for load in loads:
        load.start()

    halo = [
        (pl.ds(0, 2), pl.ds(8, 2), me - 1),
        (pl.ds(2, 2), pl.ds(10, 2), me - 1),
        (pl.ds(2, 2), pl.ds(2, 2), me + 1),
        (pl.ds(0, 2), pl.ds(0, 2), me + 1),
    ]

    def halo_copy(i):
        source, target, device = halo[i]
        return pltpu.make_async_remote_copy(
            src_ref=cond_h.at[source], dst_ref=cond.at[target],
            send_sem=halo_send.at[i], recv_sem=halo_recv.at[i],
            device_id={"slab": device},
        )

    has_low = me > 0
    has_high = me < n - 1

    @pl.when(me == 0)
    def _():
        cond[0:4] = jnp.zeros((4, SIDE, SIDE), F32)

    @pl.when(me == n - 1)
    def _():
        cond[8:12] = jnp.zeros((4, SIDE, SIDE), F32)

    row_s = lax.broadcasted_iota(jnp.int32, (SIDE, 1), 0)

    def build(planes, spots, low, count, masks):
        key = (planes[...] - low) * SIDE + lax.shift_right_logical(spots[...], 7)
        for p in range(count):
            masks[p * SIDE:(p + 1) * SIDE, :] = jnp.where(
                row_s + p * SIDE == key, 1.0, 0.0
            ).astype(BF16)
        return row_s == (spots[...] & (SIDE - 1))

    for i in range(3):
        loads[i].wait()
    here = build(sp, ss, me * DEPTH - 3, 10, mask_s)
    high = cur[...].astype(BF16).astype(F32)
    low = cur[...] - high
    columns = jnp.concatenate(
        [jnp.where(here, high, 0.0).astype(BF16), jnp.where(here, low, 0.0).astype(BF16)], axis=0
    )

    pl.semaphore_wait(barrier, peers)

    @pl.when(has_low)
    def _():
        halo_copy(0).start()

    @pl.when(has_high)
    def _():
        halo_copy(2).start()

    @pl.when(has_low)
    def _():
        halo_copy(1).start()

    @pl.when(has_high)
    def _():
        halo_copy(3).start()

    placed = dot(mask_s[...], columns, NT)
    for p in range(10):
        rows = slice(p * SIDE, (p + 1) * SIDE)
        r[p + 1] = placed[rows, 0:SIDE] + placed[rows, SIDE:2 * SIDE]

    for i in range(3, 6):
        loads[i].wait()
    here = build(rp, rs, me * DEPTH - 2, 8, mask_r)
    high = dat[...].astype(BF16).astype(F32)
    low = dat[...] - high
    columns = jnp.concatenate(
        [jnp.where(here, value, 0.0).astype(BF16) for value in (1.0, high, low)], axis=0
    )
    placed = dot(mask_r[...], columns, NT)
    for p in range(8):
        rows = slice(p * SIDE, (p + 1) * SIDE)
        cnt[p + 2] = placed[rows, 0:SIDE]
        dd[p + 2] = placed[rows, SIDE:2 * SIDE] + placed[rows, 2 * SIDE:3 * SIDE]

    for i in range(6, 12):
        loads[i].wait()

    def weigh(k):
        theta, scale = mode[0], mode[1]
        other = me - k
        other = jnp.where(other < 0, other + n, other)
        for t in range(3):
            mine = me + (t - 1)
            lower = jnp.minimum(mine, other)
            upper = jnp.maximum(mine, other)
            between = (upper - lower).astype(F32)
            below = (2 * (lower + 1)).astype(F32)
            above = (2 * (n - upper)).astype(F32)
            weight[t, k] = (
                scale
                * jnp.exp(-theta * between)
                * (1.0 - jnp.exp(-theta * below))
                * (1.0 - jnp.exp(-theta * above))
            )

    weigh(0)
    each(weigh)

    y_at = lax.broadcasted_iota(jnp.int32, (SIDE, SIDE), 0)
    z_at = lax.broadcasted_iota(jnp.int32, (SIDE, SIDE), 1)
    y_first, y_last = y_at == 0, y_at == SIDE - 1
    z_first, z_last = z_at == 0, z_at == SIDE - 1

    def back(v, axis):
        return pltpu.roll(v, 1, axis)

    def ahead(v, axis):
        return pltpu.roll(v, SIDE - 1, axis)

    def face_x(p):
        sx[p] = 0.5 * (cond[p - 1] + cond[p])

    def cell(p):
        c = cond[p]
        half = 0.5 * c
        prev_y = jnp.where(y_first, 0.0, back(half, 0))
        next_y = jnp.where(y_last, 0.0, ahead(half, 0))
        prev_z = jnp.where(z_first, 0.0, back(half, 1))
        next_z = jnp.where(z_last, 0.0, ahead(half, 1))
        sy[p] = jnp.where(y_first, 0.0, half + prev_y)
        sz[p] = jnp.where(z_first, 0.0, half + prev_z)
        total = sx[p] + sx[p + 1] + (c + prev_y + next_y) + (c + prev_z + next_z)
        if 4 <= p < 8:
            dg[p - 4] = total
            w[p] = (2.0 / 3.0) / total
        else:
            inside = has_low if p < 4 else has_high
            keep = jnp.where(inside, F32(1.0), F32(0.0))
            w[p] = keep * (2.0 / 3.0) / (total + (1.0 - keep))

    def around(v, p):
        mid = v[p]
        in_y, in_z = sy[p], sz[p]
        return (
            sx[p] * v[p - 1] + sx[p + 1] * v[p + 1]
            + (in_y * back(mid, 0) + ahead(in_y * mid, 0))
            + (in_z * back(mid, 1) + ahead(in_z * mid, 1))
        )

    lane_group = lax.broadcasted_iota(jnp.int32, (8, SIDE), 1) // COARSE

    def to_modes(field):
        left = dot(fy[...], pieces(field, 0))
        full = dot(pieces(left, 1), fz[...])
        out = jnp.zeros((8, SIDE), F32)
        for q in range(4):
            out = jnp.where(lane_group == q, full[8 * q:8 * q + 8], out)
        return out

    def from_modes(packed):
        rows = [jnp.where(lane_group == q, one, 0.0) for one in packed for q in range(4)]
        right = dot(pieces(jnp.concatenate(rows, axis=0), 1), iz[...])
        wide = jnp.concatenate([right[COARSE * t:COARSE * (t + 1)] for t in range(3)], axis=1)
        full = dot(iy[...], pieces(wide, 0))
        return [full[:, SIDE * t:SIDE * (t + 1)] for t in range(3)]

    def gather(source, target, number):
        def send(k):
            pltpu.make_async_remote_copy(
                src_ref=source, dst_ref=target.at[k - 1],
                send_sem=send_sem.at[number], recv_sem=recv_sem.at[number],
                device_id=peer(k),
            ).start()

        each(send)

    def arrived(target, number):
        pltpu.make_async_copy(target, target, recv_sem.at[number]).wait()

    def combine(own, target):
        def add(k, total):
            value = target[k - 1]
            return tuple(total[t] + weight[t, k] * value for t in range(3))

        total = tuple(weight[t, 0] * own[...] for t in range(3))
        if n <= 16:
            for k in range(1, n):
                total = add(k, total)
            return total
        return lax.fori_loop(1, n, add, total)

    def plane_of(p):
        return 0 if p < 4 else (1 if p < 8 else 2)

    @pl.when(has_high)
    def _():
        halo_copy(0).wait_recv()

    @pl.when(has_low)
    def _():
        halo_copy(2).wait_recv()

    for p in range(3, 10):
        face_x(p)
    for p in range(3, 9):
        cell(p)
        x1[p] = w[p] * r[p]
    total = None
    for p in range(4, 8):
        part = r[p] * (1.0 / 3.0) + around(x1, p)
        total = part if total is None else total + part
    spec_f[...] = to_modes(total)
    gather(spec_f, got_f, 0)

    for p in range(3, 9):
        x2[p] = w[p] * dd[p]
    total = None
    for p in range(4, 8):
        part = dd[p] * (1.0 / 3.0) + around(x2, p)
        total = part if total is None else total + part
    spec_d[...] = to_modes(total)
    gather(spec_d, got_d, 1)

    @pl.when(has_high)
    def _():
        halo_copy(1).wait_recv()

    @pl.when(has_low)
    def _():
        halo_copy(3).wait_recv()

    for p in (1, 2, 10, 11):
        face_x(p)
    for p in (1, 2, 9, 10):
        cell(p)
        x1[p] = w[p] * r[p]

    arrived(got_f, 0)
    lifted = from_modes(combine(spec_f, got_f))
    for p in range(1, 11):
        x2[p] = x1[p] + lifted[plane_of(p)]
    for p in range(2, 10):
        z = x2[p] * (1.0 / 3.0) + w[p] * (r[p] + around(x2, p))
        zfull[p] = z
        u = cnt[p] * z
        ru[p] = u
        x1[p] = w[p] * u
    total = None
    for p in range(4, 8):
        part = ru[p] * (1.0 / 3.0) + around(x1, p)
        total = part if total is None else total + part
    spec_u[...] = to_modes(total)
    gather(spec_u, got_u, 2)

    def sums(v, source):
        along = bend = None
        for p in range(4, 8):
            z = v[p]
            a = source(p) * z
            b = z * (dg[p - 4] * z - around(v, p))
            along = a if along is None else along + a
            bend = b if bend is None else bend + b
        return jnp.concatenate(
            [jnp.sum(along, axis=0, keepdims=True), jnp.sum(bend, axis=0, keepdims=True)], axis=0
        )

    def ratio(own, target):
        every = own[...] + jnp.sum(target[...], axis=0)
        both = jnp.sum(every, axis=1, keepdims=True)
        return both[0:1] / both[1:2]

    sum_a[...] = sums(zfull, lambda p: r[p])
    gather(sum_a, got_a, 3)
    stores = [
        pltpu.make_async_copy(zfull.at[pl.ds(4, 4)], zf_h, out_sem.at[0]),
        pltpu.make_async_copy(grad_o, grad_h, out_sem.at[1]),
        pltpu.make_async_copy(scal_o, scal_h, out_sem.at[2]),
    ]
    stores[0].start()

    arrived(got_d, 1)
    modes_d = combine(spec_d, got_d)
    arrived(got_a, 3)
    alpha = ratio(sum_a, got_a)
    arrived(got_u, 2)
    modes_u = combine(spec_u, got_u)
    lifted = from_modes([alpha * modes_u[t] - modes_d[t] for t in range(3)])
    for p in range(2, 10):
        ra = alpha * ru[p] - dd[p]
        r[p] = ra
        x2[p] = w[p] * ra + lifted[plane_of(p)]
    for p in range(3, 9):
        za[p] = x2[p] * (1.0 / 3.0) + w[p] * (r[p] + around(x2, p))
    sum_b[...] = sums(za, lambda p: r[p])
    gather(sum_b, got_b, 4)

    def face_pairs(f, a, first, last, axis):
        step_f = f - jnp.where(first, 0.0, back(f, axis))
        step_a = a - jnp.where(first, 0.0, back(a, axis))
        product = step_f * step_a
        return product + jnp.where(last, f * a, ahead(product, axis))

    lower = (zfull[4] - zfull[3]) * (za[4] - za[3])
    for p in range(4, 8):
        f, a = zfull[p], za[p]
        upper = (zfull[p + 1] - f) * (za[p + 1] - a)
        grad_o[p - 4] = (
            lower + upper
            + face_pairs(f, a, y_first, y_last, 0)
            + face_pairs(f, a, z_first, z_last, 1)
        )
        lower = upper
    stores[1].start()

    @pl.when(has_low)
    def _():
        halo_copy(0).wait_send()
        halo_copy(1).wait_send()

    @pl.when(has_high)
    def _():
        halo_copy(2).wait_send()
        halo_copy(3).wait_send()

    for number, target in enumerate((got_f, got_d, got_u, got_a)):
        pltpu.make_async_copy(target, target, send_sem.at[number]).wait()
    arrived(got_b, 4)
    beta = ratio(sum_b, got_b)
    at = lax.broadcasted_iota(jnp.int32, (8, SIDE), 0)
    scal_o[...] = jnp.where(at == 0, alpha, -0.5 * alpha * beta)
    stores[2].start()
    pltpu.make_async_copy(got_b, got_b, send_sem.at[4]).wait()
    for store in stores:
        store.wait()


def scale_kernel(zf, grad, scal, potential, gradient, held, ready, factors, load_sem, sem):
    loads = [
        pltpu.make_async_copy(scal, factors, load_sem.at[0]),
        pltpu.make_async_copy(zf, held.at[pl.ds(0, DEPTH)], load_sem.at[1]),
        pltpu.make_async_copy(grad, held.at[pl.ds(DEPTH, DEPTH)], load_sem.at[2]),
    ]
    for load in loads:
        load.start()
    loads[0].wait()
    copies = []
    for row, target in enumerate((potential.at[0], gradient)):
        loads[row + 1].wait()
        factor = jnp.broadcast_to(factors[row:row + 1, :], (SIDE, SIDE))
        for p in range(DEPTH):
            at = row * DEPTH + p
            ready[at] = factor * held[at]
            copies.append(pltpu.make_async_copy(ready.at[at], target.at[p], sem.at[at]))
            copies[-1].start()
    for copy in copies:
        copy.wait()


def on_device(n, cond, *rest):
    elec, recv = rest[0].shape[1], rest[3].shape[1]
    consts = tables(n)
    cube = lambda count: pltpu.VMEM((count, SIDE, SIDE), F32)
    vreg = pltpu.VMEM((8, SIDE), F32)
    pair = pltpu.VMEM((2, SIDE), F32)
    field = jax.ShapeDtypeStruct((DEPTH, SIDE, SIDE), F32)
    scratch = (
        [cube(12)]
        + [pltpu.VMEM(a.shape, a.dtype) for a in rest]
        + [pltpu.VMEM(a.shape, a.dtype) for a in consts]
        + [pltpu.VMEM((10 * SIDE, elec), BF16), pltpu.VMEM((8 * SIDE, recv), BF16)]
        + [cube(12), cube(12), cube(12), cube(4)]
        + [cube(12)] * 9
        + [pltpu.VMEM((3, n, 8, SIDE), F32)]
        + [cube(DEPTH), vreg]
        + [vreg] * 3 + [pair] * 2
        + [pltpu.VMEM((n - 1, 8, SIDE), F32)] * 3
        + [pltpu.VMEM((n - 1, 2, SIDE), F32)] * 2
        + [
            pltpu.SemaphoreType.DMA((12,)),
            pltpu.SemaphoreType.DMA((3,)),
            pltpu.SemaphoreType.DMA((4,)),
            pltpu.SemaphoreType.DMA((4,)),
            pltpu.SemaphoreType.DMA((5,)),
            pltpu.SemaphoreType.DMA((5,)),
        ]
    )
    zf, grad, scal = pl.pallas_call(
        functools.partial(kernel, n),
        out_shape=(field, field, jax.ShapeDtypeStruct((8, SIDE), F32)),
        in_specs=[pl.BlockSpec(memory_space=pl.ANY)] * 12,
        out_specs=[pl.BlockSpec(memory_space=pl.ANY)] * 3,
        scratch_shapes=scratch,
        compiler_params=pltpu.CompilerParams(
            collective_id=0, has_side_effects=True, vmem_limit_bytes=VMEM_BYTES
        ),
    )(cond, *rest, *[jnp.asarray(c) for c in consts])
    return pl.pallas_call(
        scale_kernel,
        out_shape=(jax.ShapeDtypeStruct((1, DEPTH, SIDE, SIDE), F32), field),
        in_specs=[pl.BlockSpec(memory_space=pl.ANY)] * 3,
        out_specs=[pl.BlockSpec(memory_space=pl.ANY)] * 2,
        scratch_shapes=[
            cube(2 * DEPTH), cube(2 * DEPTH), vreg,
            pltpu.SemaphoreType.DMA((3,)), pltpu.SemaphoreType.DMA((2 * DEPTH,)),
        ],
        compiler_params=pltpu.CompilerParams(vmem_limit_bytes=VMEM_BYTES),
    )(zf, grad, scal)


def solution(mesh):
    in_specs = (P(("survey", "slab"), None, None),) + (P("survey", None),) * 6
    out_specs = (P("survey", "slab", None, None), P(("survey", "slab"), None, None))
    return jax.shard_map(
        functools.partial(on_device, mesh.shape["slab"]),
        mesh=mesh, in_specs=in_specs, out_specs=out_specs, check_vma=False,
    )
```
